32 devices in a mesh: fsdp: 32 (over z, y, x, core).
Axes of the slice: x: 2, y: 2, z: 4, core: 2. Of those that a mesh axis runs over, the one named last changes fastest.
Arguments:
- tokens: float32 [160, 196, 512], P('fsdp'), may hold values from -6 to 6
- live_count: int32 [32], P('fsdp'), may hold values from 4 to 5, as said below
- rel_index: int32 [49, 49], replicated, may hold values from 0 to 175, as said below
- mask_ids: int32 [196], replicated, may hold values from 0 to 8, as said below
- norm1_gain: bfloat16 [2, 512], P(None, 'fsdp'), may hold values from 0.5 to 1.5
- norm1_bias: bfloat16 [2, 512], P(None, 'fsdp'), may hold values from -4 to 4
- qkv_weight: bfloat16 [2, 512, 1536], P(None, 'fsdp'), may hold values from -0.25 to 0.25
- qv_bias: bfloat16 [2, 1024], P(None, 'fsdp'), may hold values from -4 to 4
- bias_table: bfloat16 [2, 2816], P(None, 'fsdp'), may hold values from -4 to 4
- proj_weight: bfloat16 [2, 512, 512], P(None, 'fsdp'), may hold values from -1.5 to 1.5
- proj_bias: bfloat16 [2, 512], P(None, 'fsdp'), may hold values from -4 to 4
- norm2_gain: bfloat16 [2, 512], P(None, 'fsdp'), may hold values from 0.5 to 1.5
- norm2_bias: bfloat16 [2, 512], P(None, 'fsdp'), may hold values from -4 to 4
- fc1_weight: bfloat16 [2, 512, 2048], P(None, 'fsdp'), may hold values from -0.25 to 0.25
- fc1_bias: bfloat16 [2, 2048], P(None, 'fsdp'), may hold values from -4 to 4
- fc2_weight: bfloat16 [2, 2048, 512], P(None, 'fsdp'), may hold values from -0.125 to 0.125
- fc2_bias: bfloat16 [2, 512], P(None, 'fsdp'), may hold values from -4 to 4
- cotangent: float32 [160, 196, 512], P('fsdp'), may hold values from -6 to 6
Outputs:
- result: float32 [160, 196, 512], P('fsdp')
- tokens_grad: float32 [160, 196, 512], P('fsdp')
- norm1_gain_grad: float32 [2, 512], P(None, 'fsdp')
- norm1_bias_grad: float32 [2, 512], P(None, 'fsdp')
- qkv_weight_grad: float32 [2, 512, 1536], P(None, 'fsdp')
- qv_bias_grad: float32 [2, 1024], P(None, 'fsdp')
- bias_table_grad: float32 [2, 2816], P(None, 'fsdp')
- proj_weight_grad: float32 [2, 512, 512], P(None, 'fsdp')
- proj_bias_grad: float32 [2, 512], P(None, 'fsdp')
- norm2_gain_grad: float32 [2, 512], P(None, 'fsdp')
- norm2_bias_grad: float32 [2, 512], P(None, 'fsdp')
- fc1_weight_grad: float32 [2, 512, 2048], P(None, 'fsdp')
- fc1_bias_grad: float32 [2, 2048], P(None, 'fsdp')
- fc2_weight_grad: float32 [2, 2048, 512], P(None, 'fsdp')
- fc2_bias_grad: float32 [2, 512], P(None, 'fsdp')
The draws below stay inside these ranges and needn't reach their ends.
Inputs may be any that keep to these rules, and one draw needn't show every extreme that they name: Device i holds live_count[i] live images in its first slots of tokens; the rest of its 5 slots are empty. Some device holds 5 live images and some 4. `rel_index`: query and key position pairs of a window with the same offset in rows and columns name the same row of the bias table, pairs with different offsets different rows; rows 0 and 175 are always named. `mask_ids`: positions of the rolled grid in one of the nine regions that the roll by 3 makes (three bands of rows times three bands of columns) share a label; different regions may share a label too; the first region is labelled 0 and the last 8.
All inputs are finite; a program needn't handle non-finite values.
Results may differ from the reference program's by a relative error of at most 0.015.
Values may be sent and summed in bfloat16 or wider, within the bound.
A program may use at most 256 MiB of HBM per device.

```python
import jax
import jax.numpy as jnp
from jax import lax

D = 512
FF = 2048
HEAD = 32
WIN = 7
GRID = 14
TABLE = 176
LAYERS = 2
IMG_DEV = 4
HEADS = 16
SHIFT = 3
SLOTS = 5
IMAGES = 160
N_FSDP = 32


def draw_live_count(key, part):
    key = jax.random.fold_in(key, 11)
    key_one, key_two, key_three = jax.random.split(key, 3)
    devices = IMAGES // SLOTS
    extra_one = jax.random.randint(key_one, (devices,), 0, 2)
    full_at = jax.random.randint(key_two, (), 0, devices)
    empty_at = (full_at + 1 + jax.random.randint(key_three, (), 0, devices - 1)) % devices
    places = jnp.arange(devices)
    extra_one = jnp.where(places == full_at, 1, jnp.where(places == empty_at, 0, extra_one))
    return (IMG_DEV + extra_one).astype(jnp.int32)


def draw_rel_index(key, part):
    key = jax.random.fold_in(key, 23)
    key_one, key_two = jax.random.split(key)
    offsets_used = (2 * WIN - 1) ** 2
    middle = jax.random.permutation(key_one, TABLE - 2)[:offsets_used - 2].astype(jnp.int32) + 1
    chosen = jnp.concatenate([jnp.array([0, TABLE - 1], jnp.int32), middle])
    row_of_offset = chosen[jax.random.permutation(key_two, offsets_used)]
    position = jnp.arange(WIN * WIN).astype(jnp.int32)
    place_row = position // WIN
    place_col = position % WIN
    offset = (place_row[:, None] - place_row[None, :] + WIN - 1) * (2 * WIN - 1) + (place_col[:, None] - place_col[None, :] + WIN - 1)
    return row_of_offset[offset].astype(jnp.int32)


def draw_mask_ids(key, part):
    key = jax.random.fold_in(key, 37)
    labels = jax.random.randint(key, (9,), 0, 9).astype(jnp.int32)
    spots = jnp.arange(9)
    labels = jnp.where(spots == 0, 0, jnp.where(spots == 8, 8, labels))
    lines = jnp.arange(GRID)
    band = jnp.where(lines < GRID - WIN, 0, jnp.where(lines < GRID - SHIFT, 1, 2))
    region = band[:, None] * 3 + band[None, :]
    return labels[region.reshape(-1)].astype(jnp.int32)


def with_spikes(values, key, source, target, parts, factor):
    owner, partner = [(jnp.arange(values.shape[dim]) // (values.shape[dim] // parts)).reshape([-1 if axis == dim else 1 for axis in range(values.ndim)]) for dim in (source, target)]
    chosen = jax.random.permutation(key, parts)[partner]
    strong = (owner == chosen) | (owner == (partner + parts // 2) % parts)
    return jnp.where(strong, factor * values, values)


def levels(key, shape, cuts, least, largest):
    loudness = 1.0
    for dim, shards_of in cuts:
        draws = jax.random.uniform(jax.random.fold_in(jax.random.fold_in(key, 6), dim), (shards_of,), jnp.float32, least / len(cuts), largest / len(cuts))
        loudness = loudness * jnp.repeat(jnp.exp(draws), shape[dim] // shards_of).reshape((-1,) + (1,) * (len(shape) - 1 - dim))
    return loudness


def bell_draw(stream_key, extent, spread, most, cuts=(), held_as=jnp.bfloat16):
    factor_of = levels(stream_key, extent, cuts, -0.22, 0.18) if cuts else 1.0
    entries = jax.random.normal(stream_key, extent, jnp.float32) * spread * factor_of
    return jnp.minimum(jnp.maximum(entries, -most), most).astype(held_as)


def gaussian_with(own_key, extent, spread, reach, cuts, heavy, kind=jnp.bfloat16):
    result = spread * jax.random.normal(own_key, extent, jnp.float32)
    if cuts:
        result = result * levels(own_key, extent, cuts, -0.22, 0.18)
    return jnp.clip(with_spikes(result, jax.random.fold_in(own_key, 3), *heavy), -reach, reach).astype(kind)


def setup_inputs(seed: int = 0) -> dict:
    key_list = jax.random.split(jax.random.key(seed), 19)
    tokens = bell_draw(key_list[0], (IMAGES, GRID * GRID, D), 1.0, 6.0, ((0, 32),), jnp.float32)
    live_count = draw_live_count(jax.random.fold_in(key_list[18], 71), 0)
    rel_index = draw_rel_index(jax.random.fold_in(key_list[18], 71), 0)
    mask_ids = draw_mask_ids(jax.random.fold_in(key_list[18], 71), 0)
    norm1_gain = jnp.clip(1.0 + 0.1 * jax.random.normal(key_list[4], (LAYERS, D), jnp.float32), 0.5, 1.5).astype(jnp.bfloat16)
    norm1_bias = bell_draw(key_list[5], (LAYERS, D), 0.3, 4.0, ((1, 32),))
    qkv_weight = bell_draw(key_list[6], (LAYERS, D, 3 * D), D ** -0.5, 0.25, ((1, 32),))
    qv_bias = bell_draw(key_list[7], (LAYERS, 2 * D), 0.3, 4.0, ((1, 32),))
    bias_table = bell_draw(key_list[8], (LAYERS, TABLE * HEADS), 1.0, 4.0, ((1, 32),))
    proj_weight = bell_draw(key_list[9], (LAYERS, D, D), (D // 32) ** -0.5, 1.5, ((1, 32),))
    proj_bias = bell_draw(key_list[10], (LAYERS, D), 0.3, 4.0, ((1, 32),))
    norm2_gain = jnp.clip(1.0 + 0.1 * jax.random.normal(key_list[11], (LAYERS, D), jnp.float32), 0.5, 1.5).astype(jnp.bfloat16)
    norm2_bias = bell_draw(key_list[12], (LAYERS, D), 0.3, 4.0, ((1, 32),))
    fc1_weight = bell_draw(key_list[13], (LAYERS, D, FF), D ** -0.5, 0.25, ((1, 32),))
    fc1_bias = bell_draw(key_list[14], (LAYERS, FF), 0.3, 4.0, ((1, 32),))
    fc2_weight = bell_draw(key_list[15], (LAYERS, FF, D), FF ** -0.5, 0.125, ((1, 32),))
    fc2_bias = bell_draw(key_list[16], (LAYERS, D), 0.3, 4.0, ((1, 32),))
    cotangent = gaussian_with(key_list[17], (IMAGES, GRID * GRID, D), 1.0, 6.0, ((0, 32),), (0, 2, 32, 2.75), jnp.float32)
    return dict(tokens=tokens, live_count=live_count, rel_index=rel_index, mask_ids=mask_ids, norm1_gain=norm1_gain, norm1_bias=norm1_bias, qkv_weight=qkv_weight, qv_bias=qv_bias, bias_table=bias_table, proj_weight=proj_weight, proj_bias=proj_bias, norm2_gain=norm2_gain, norm2_bias=norm2_bias, fc1_weight=fc1_weight, fc1_bias=fc1_bias, fc2_weight=fc2_weight, fc2_bias=fc2_bias, cotangent=cotangent)


@jax.custom_vjp
def low(v):
    return lax.optimization_barrier(v.astype(jnp.bfloat16)).astype(jnp.float32)

@jax.custom_vjp
def low_back(v):
    return v

def low_keep(v):
    return (low(v), None)

def low_pass(kept, grad):
    return (grad,)

def back_keep(v):
    return (v, None)

def back_low(kept, grad):
    return (low(grad),)
low.defvjp(low_keep, low_pass)
low_back.defvjp(back_keep, back_low)
norm_eps = 1e-05
mask_fill = -100.0
highest = lax.Precision.HIGHEST

def to_windows(grid_rows):
    images = grid_rows.shape[0]
    features = grid_rows.shape[-1]
    split = grid_rows.reshape(images, GRID // WIN, WIN, GRID // WIN, WIN, features)
    split = split.transpose(0, 1, 3, 2, 4, 5)
    return split.reshape(images * (GRID // WIN) ** 2, WIN * WIN, features)

def from_windows(windows, images):
    features = windows.shape[-1]
    split = windows.reshape(images, GRID // WIN, GRID // WIN, WIN, WIN, features)
    split = split.transpose(0, 1, 3, 2, 4, 5)
    return split.reshape(images, GRID, GRID, features)

def enter_windows(token_rows, shifted):
    images = token_rows.shape[0]
    grid_rows = token_rows.reshape(images, GRID, GRID, token_rows.shape[-1])
    if shifted:
        grid_rows = jnp.roll(grid_rows, (-SHIFT, -SHIFT), axis=(1, 2))
    return to_windows(grid_rows)

def leave_windows(windows, images, shifted):
    grid_rows = from_windows(windows, images)
    if shifted:
        grid_rows = jnp.roll(grid_rows, (SHIFT, SHIFT), axis=(1, 2))
    return grid_rows.reshape(images, GRID * GRID, windows.shape[-1])

def layer_norm(stream, gain_row, offset):
    average = lax.optimization_barrier(jnp.mean(stream, axis=-1, keepdims=True))
    centred = stream - average
    variance = lax.optimization_barrier(jnp.mean(centred * centred, axis=-1, keepdims=True))
    return centred * lax.rsqrt(variance + norm_eps) * gain_row + offset

def swin_layer(stream, weights, shifted, rel_index, region):
    gain_one, offset_one, qkv_w, qv_b, table_flat, proj_w, proj_b, gain_two, offset_two, up_w, up_b, down_w, down_b = weights
    images = stream.shape[0]
    features = stream.shape[-1]
    normed_one = low(layer_norm(stream, gain_one, offset_one))
    windows = enter_windows(normed_one, shifted)
    window_count = windows.shape[0]
    qkv = low_back(jnp.einsum('wtd,de->wte', windows, qkv_w, precision=highest))
    qkv = qkv + jnp.concatenate([qv_b[:features], jnp.zeros((features,), jnp.float32), qv_b[features:]])
    head_scale = HEAD ** (-0.5)
    head_shape = (window_count, WIN * WIN, HEADS, HEAD)
    queries = low(qkv[..., :features] * head_scale).reshape(head_shape)
    keys_low = low(qkv[..., features:2 * features]).reshape(head_shape)
    values_low = low(qkv[..., 2 * features:]).reshape(head_shape)
    logits = low_back(jnp.einsum('wqhc,wkhc->whqk', queries, keys_low, precision=highest))
    bias_heads = table_flat.reshape(TABLE, HEADS)[rel_index].transpose(2, 0, 1)
    scores = logits + bias_heads[None]
    if shifted:
        mask_add = jnp.where(region[:, :, None] == region[:, None, :], 0.0, mask_fill)
        per_image = mask_add.shape[0]
        scores = (scores.reshape(window_count // per_image, per_image, HEADS, WIN * WIN, WIN * WIN) + mask_add[None, :, None]).reshape(scores.shape)
    attn_probs = low(jax.nn.softmax(scores, axis=-1))
    attended = jnp.einsum('whqk,wkhc->wqhc', attn_probs, values_low, precision=highest)
    attended = low(low_back(attended.reshape(window_count, WIN * WIN, features)))
    projected = low_back(jnp.einsum('wtd,de->wte', attended, proj_w, precision=highest)) + proj_b
    stream_mid = stream + leave_windows(projected, images, shifted)
    normed_two = low(layer_norm(stream_mid, gain_two, offset_two))
    hidden_pre = low_back(jnp.einsum('std,de->ste', normed_two, up_w, precision=highest)) + up_b
    activ_low = low(jax.nn.gelu(hidden_pre, approximate=False))
    branch_out = low_back(jnp.einsum('ste,ed->std', activ_low, down_w, precision=highest)) + down_b
    return stream_mid + branch_out

def forward(stream, live_rows, weights_all, rel_index, region):
    for layer_index in range(LAYERS):
        weights = tuple((weight[layer_index] for weight in weights_all))
        stream = swin_layer(stream, weights, layer_index % 2 == 1, rel_index, region)
    return stream * live_rows[:, None, None]

def reference(tokens, live_count, rel_index, mask_ids, norm1_gain, norm1_bias, qkv_weight, qv_bias, bias_table, proj_weight, proj_bias, norm2_gain, norm2_bias, fc1_weight, fc1_bias, fc2_weight, fc2_bias, cotangent):
    weights_all = tuple((weight.astype(jnp.float32) for weight in (norm1_gain, norm1_bias, qkv_weight, qv_bias, bias_table, proj_weight, proj_bias, norm2_gain, norm2_bias, fc1_weight, fc1_bias, fc2_weight, fc2_bias)))
    slot_total = tokens.shape[0]
    slot_place = jnp.arange(slot_total).astype(jnp.int32)
    live = (slot_place % SLOTS < jnp.repeat(live_count, SLOTS)).astype(jnp.float32)
    region = to_windows(mask_ids.reshape(1, GRID, GRID, 1)).reshape(-1, WIN * WIN)
    target = max(1, 4096 // (SLOTS * GRID * GRID))
    devices_step = 1
    while devices_step * 2 <= target and N_FSDP % (devices_step * 2) == 0:
        devices_step = devices_step * 2
    group_size = devices_step * SLOTS
    rounds = slot_total // group_size

    def one_group(grad_totals, pieces):
        stream, live_rows, cot_rows = pieces

        def run_group(stream_in, weights_in):
            return forward(stream_in, live_rows, weights_in, rel_index, region)
        result_rows, pullback = jax.vjp(run_group, stream, weights_all)
        stream_grad, weight_grads = pullback(cot_rows)
        grad_totals = tuple((total_grad + new_grad for total_grad, new_grad in zip(grad_totals, weight_grads)))
        return (grad_totals, (result_rows, stream_grad))
    zero_grads = tuple((jnp.zeros_like(weight) for weight in weights_all))
    shape_rows = (rounds, group_size) + tokens.shape[1:]
    grad_totals, (results, stream_grads) = lax.scan(one_group, zero_grads, (tokens.reshape(shape_rows), live.reshape(rounds, group_size), cotangent.reshape(shape_rows)))
    return (results.reshape(tokens.shape), stream_grads.reshape(tokens.shape), grad_totals[0], grad_totals[1], grad_totals[2], grad_totals[3], grad_totals[4], grad_totals[5], grad_totals[6], grad_totals[7], grad_totals[8], grad_totals[9], grad_totals[10], grad_totals[11], grad_totals[12])
```

```python
import functools

import jax
import jax.numpy as jnp
from jax import lax
from jax.sharding import PartitionSpec as P

HEAD = 32
WIN = 7
GRID = 14
TABLE = 176
LAYERS = 2
HEADS = 16
SHIFT = 3


norm_eps = 1e-05
mask_fill = -100.0


def to_windows(grid_rows):
    images = grid_rows.shape[0]
    features = grid_rows.shape[-1]
    split = grid_rows.reshape(images, GRID // WIN, WIN, GRID // WIN, WIN, features)
    split = split.transpose(0, 1, 3, 2, 4, 5)
    return split.reshape(images * (GRID // WIN) ** 2, WIN * WIN, features)


def from_windows(windows, images):
    features = windows.shape[-1]
    split = windows.reshape(images, GRID // WIN, GRID // WIN, WIN, WIN, features)
    split = split.transpose(0, 1, 3, 2, 4, 5)
    return split.reshape(images, GRID, GRID, features)


def enter_windows(token_rows, shifted):
    images = token_rows.shape[0]
    grid_rows = token_rows.reshape(images, GRID, GRID, token_rows.shape[-1])
    if shifted:
        grid_rows = jnp.roll(grid_rows, (-SHIFT, -SHIFT), axis=(1, 2))
    return to_windows(grid_rows)


def leave_windows(windows, images, shifted):
    grid_rows = from_windows(windows, images)
    if shifted:
        grid_rows = jnp.roll(grid_rows, (SHIFT, SHIFT), axis=(1, 2))
    return grid_rows.reshape(images, GRID * GRID, windows.shape[-1])


def layer_norm(stream, gain_row, offset):
    average = jnp.mean(stream, axis=-1, keepdims=True)
    centred = stream - average
    variance = jnp.mean(centred * centred, axis=-1, keepdims=True)
    return centred * lax.rsqrt(variance + norm_eps) * gain_row + offset


def gelu_exact(hidden):
    return jax.nn.gelu(hidden, approximate=False)


def contract_rows(rows_left, rows_right, precision=None):
    return lax.dot_general(
        rows_left,
        rows_right,
        (((0,), (0,)), ((), ())),
        precision=precision,
        preferred_element_type=jnp.float32,
    )


def times_transposed(rows_left, rows_right):
    return lax.dot_general(
        rows_left, rows_right, (((1,), (1,)), ((), ())), preferred_element_type=jnp.float32
    )


def position_bias(table_flat, rel_onehot):
    table_rows = table_flat.astype(jnp.float32).reshape(TABLE, HEADS)
    lookup = jnp.dot(
        rel_onehot, table_rows, precision=lax.Precision.HIGHEST, preferred_element_type=jnp.float32
    )
    return lookup.reshape(WIN * WIN, WIN * WIN, HEADS).transpose(2, 0, 1)


def attend_scores(queries, keys_low, bias_heads, mask_add):
    scores = jnp.einsum("wqhc,wkhc->whqk", queries, keys_low, preferred_element_type=jnp.float32)
    scores = scores + bias_heads[None]
    if mask_add is not None:
        window_count = scores.shape[0]
        per_image = mask_add.shape[0]
        scores = (
            scores.reshape(window_count // per_image, per_image, HEADS, WIN * WIN, WIN * WIN)
            + mask_add[None, :, None]
        ).reshape(scores.shape)
    return scores


def layer_forward(stream, weights, shifted, rel_onehot, mask_add):
    (
        gain_one,
        offset_one,
        qkv_w,
        qv_b,
        table_flat,
        proj_w,
        proj_b,
        gain_two,
        offset_two,
        up_w,
        up_b,
        down_w,
        down_b,
    ) = weights
    images = stream.shape[0]
    features = stream.shape[-1]
    normed_one = layer_norm(
        stream, gain_one.astype(jnp.float32), offset_one.astype(jnp.float32)
    ).astype(jnp.bfloat16)
    windows = enter_windows(normed_one, shifted).reshape(-1, features)
    window_count = windows.shape[0] // (WIN * WIN)
    qv_float = qv_b.astype(jnp.float32)
    qkv = jnp.dot(windows, qkv_w, preferred_element_type=jnp.float32)
    qkv = qkv + jnp.concatenate(
        [qv_float[:features], jnp.zeros((features,), jnp.float32), qv_float[features:]]
    )
    head_shape = (window_count, WIN * WIN, HEADS, HEAD)
    head_scale = HEAD ** (-0.5)
    queries = (qkv[:, :features] * head_scale).astype(jnp.bfloat16).reshape(head_shape)
    keys_low = qkv[:, features : 2 * features].astype(jnp.bfloat16).reshape(head_shape)
    values_low = qkv[:, 2 * features :].astype(jnp.bfloat16).reshape(head_shape)
    scores = attend_scores(queries, keys_low, position_bias(table_flat, rel_onehot), mask_add)
    row_top = jnp.max(scores, axis=-1, keepdims=True)
    log_total = row_top + jnp.log(jnp.sum(jnp.exp(scores - row_top), axis=-1, keepdims=True))
    probs_low = jnp.exp(scores - log_total).astype(jnp.bfloat16)
    attended = jnp.einsum(
        "whqk,wkhc->wqhc", probs_low, values_low, preferred_element_type=jnp.float32
    )
    attended = attended.astype(jnp.bfloat16).reshape(-1, features)
    projected = jnp.dot(attended, proj_w, preferred_element_type=jnp.float32) + proj_b.astype(
        jnp.float32
    )
    stream_mid = stream + leave_windows(
        projected.reshape(window_count, WIN * WIN, features), images, shifted
    )
    normed_two = layer_norm(
        stream_mid, gain_two.astype(jnp.float32), offset_two.astype(jnp.float32)
    ).astype(jnp.bfloat16)
    hidden_pre = jnp.dot(
        normed_two.reshape(-1, features), up_w, preferred_element_type=jnp.float32
    ) + up_b.astype(jnp.float32)
    activ_low = gelu_exact(hidden_pre).astype(jnp.bfloat16)
    branch_out = jnp.dot(activ_low, down_w, preferred_element_type=jnp.float32) + down_b.astype(
        jnp.float32
    )
    output = stream_mid + branch_out.reshape(stream.shape)
    saved_state = (
        stream,
        windows,
        queries,
        keys_low,
        values_low,
        log_total,
        attended,
        stream_mid,
        normed_two,
        hidden_pre,
        activ_low,
    )
    return (output, saved_state)


def layer_backward(grad_out, saved_state, weights, shifted, rel_onehot, mask_add):
    (
        gain_one,
        offset_one,
        qkv_w,
        qv_b,
        table_flat,
        proj_w,
        proj_b,
        gain_two,
        offset_two,
        up_w,
        up_b,
        down_w,
        down_b,
    ) = weights
    (
        stream,
        windows,
        queries,
        keys_low,
        values_low,
        log_total,
        attended,
        stream_mid,
        normed_two,
        hidden_pre,
        activ_low,
    ) = saved_state
    images = stream.shape[0]
    features = stream.shape[-1]
    window_count = windows.shape[0] // (WIN * WIN)
    grad_rows = grad_out.reshape(-1, features)
    grad_down_b = jnp.sum(grad_rows, axis=0)
    grad_low = grad_rows.astype(jnp.bfloat16)
    grad_down_w = contract_rows(activ_low, grad_low)
    grad_activ = times_transposed(grad_low, down_w)
    gelu_pull = jax.vjp(gelu_exact, hidden_pre)[1]
    grad_hidden = gelu_pull(grad_activ)[0]
    grad_up_b = jnp.sum(grad_hidden, axis=0)
    grad_hidden_low = grad_hidden.astype(jnp.bfloat16)
    grad_up_w = contract_rows(normed_two.reshape(-1, features), grad_hidden_low)
    grad_normed_two = times_transposed(grad_hidden_low, up_w).reshape(stream.shape)
    norm_pull = jax.vjp(
        layer_norm, stream_mid, gain_two.astype(jnp.float32), offset_two.astype(jnp.float32)
    )[1]
    part_mid, grad_gain_two, grad_offset_two = norm_pull(grad_normed_two)
    grad_mid = grad_out + part_mid
    grad_proj = enter_windows(grad_mid, shifted).reshape(-1, features)
    grad_proj_b = jnp.sum(grad_proj, axis=0)
    grad_proj_low = grad_proj.astype(jnp.bfloat16)
    grad_proj_w = contract_rows(attended, grad_proj_low)
    head_shape = (window_count, WIN * WIN, HEADS, HEAD)
    grad_attended = times_transposed(grad_proj_low, proj_w).astype(jnp.bfloat16).reshape(head_shape)
    scores = attend_scores(queries, keys_low, position_bias(table_flat, rel_onehot), mask_add)
    attn_probs = jnp.exp(scores - log_total)
    probs_low = attn_probs.astype(jnp.bfloat16)
    grad_values = jnp.einsum(
        "whqk,wqhc->wkhc", probs_low, grad_attended, preferred_element_type=jnp.float32
    )
    grad_probs = jnp.einsum(
        "wqhc,wkhc->whqk", grad_attended, values_low, preferred_element_type=jnp.float32
    )
    grad_scores = attn_probs * (
        grad_probs - jnp.sum(grad_probs * attn_probs, axis=-1, keepdims=True)
    )
    bias_sum = jnp.sum(grad_scores, axis=0).transpose(1, 2, 0).reshape(WIN * WIN * WIN * WIN, HEADS)
    grad_table = contract_rows(rel_onehot, bias_sum, lax.Precision.HIGHEST).reshape(-1)
    grad_scores_low = grad_scores.astype(jnp.bfloat16)
    head_scale = HEAD ** (-0.5)
    grad_queries = (
        jnp.einsum("whqk,wkhc->wqhc", grad_scores_low, keys_low, preferred_element_type=jnp.float32)
        * head_scale
    )
    grad_keys = jnp.einsum(
        "whqk,wqhc->wkhc", grad_scores_low, queries, preferred_element_type=jnp.float32
    )
    grad_qkv = jnp.concatenate(
        [
            grad_queries.reshape(-1, features),
            grad_keys.reshape(-1, features),
            grad_values.reshape(-1, features),
        ],
        axis=1,
    )
    grad_qv_b = jnp.concatenate(
        [jnp.sum(grad_qkv[:, :features], axis=0), jnp.sum(grad_qkv[:, 2 * features :], axis=0)]
    )
    grad_qkv_low = grad_qkv.astype(jnp.bfloat16)
    grad_qkv_w = contract_rows(windows, grad_qkv_low)
    grad_normed_one = leave_windows(
        times_transposed(grad_qkv_low, qkv_w).reshape(window_count, WIN * WIN, features),
        images,
        shifted,
    )
    norm_pull = jax.vjp(
        layer_norm, stream, gain_one.astype(jnp.float32), offset_one.astype(jnp.float32)
    )[1]
    part_in, grad_gain_one, grad_offset_one = norm_pull(grad_normed_one)
    grad_in = grad_mid + part_in
    return (
        grad_in,
        (
            grad_gain_one,
            grad_offset_one,
            grad_qkv_w,
            grad_qv_b,
            grad_table,
            grad_proj_w,
            grad_proj_b,
            grad_gain_two,
            grad_offset_two,
            grad_up_w,
            grad_up_b,
            grad_down_w,
            grad_down_b,
        ),
    )


def bit_order(device_bits, turn):
    order = list(range(device_bits))
    if turn == 1 and device_bits > 2:
        order[1], order[2] = order[2], order[1]
    if turn == 2 and device_bits > 3:
        order[1:4] = [order[3], order[1], order[2]]
    return order


def partner_pairs(devices, bit):
    return [(place, place ^ (1 << bit)) for place in range(devices)]


def my_bit(bit):
    return (lax.axis_index("fsdp") >> bit) & 1


def gather_blocks(block, devices, turn):
    device_bits = devices.bit_length() - 1
    held = []
    for bit in reversed(bit_order(device_bits, turn)):
        other = lax.ppermute(block, "fsdp", partner_pairs(devices, bit))
        place = sum(1 for done in held if done > bit)
        held.append(bit)
        mine = my_bit(bit) == 0
        block = jnp.stack(
            [jnp.where(mine, block, other), jnp.where(mine, other, block)], axis=place
        )
    return block.reshape((devices,) + block.shape[device_bits:])


def scatter_sums(blocks, devices, turn, wire):
    device_bits = devices.bit_length() - 1
    rest = blocks.shape[1:]
    total = blocks.reshape((2,) * device_bits + rest)
    left = list(range(device_bits - 1, -1, -1))
    for bit in bit_order(device_bits, turn):
        axis = left.index(bit)
        left.remove(bit)
        mine = my_bit(bit)
        away = lax.dynamic_index_in_dim(total, 1 - mine, axis, keepdims=False).astype(wire)
        kept = lax.dynamic_index_in_dim(total, mine, axis, keepdims=False)
        arrived = lax.ppermute(away, "fsdp", partner_pairs(devices, bit))
        total = kept.astype(jnp.float32) + arrived.astype(jnp.float32)
        if left:
            total = total.astype(wire)
    return total


def shards(
    devices,
    tokens,
    live_count,
    rel_index,
    mask_ids,
    *params_and_cotangent,
):
    params = params_and_cotangent[:13]
    cotangent = params_and_cotangent[13]
    images = tokens.shape[0]
    live_rows = (jnp.arange(images) < live_count[0]).astype(jnp.float32)[:, None, None]
    rel_onehot = (rel_index.reshape(-1)[:, None] == jnp.arange(TABLE)[None, :]).astype(jnp.float32)
    region = to_windows(mask_ids.reshape(1, GRID, GRID, 1)).reshape(-1, WIN * WIN)
    mask_add = jnp.where(region[:, :, None] == region[:, None, :], 0.0, mask_fill).astype(
        jnp.float32
    )
    wide = (2, 5, 9, 11)
    narrow = tuple(member for member in range(13) if member not in wide)
    widths = [params[member].shape[1] for member in narrow]
    starts = [sum(widths[:place]) for place in range(len(widths))]
    small_all = gather_blocks(
        jnp.concatenate([params[member] for member in narrow], axis=1), devices, 1
    )
    weights_all = []
    for layer_index in range(LAYERS):
        weights = [None] * 13
        for turn, member in enumerate(wide):
            gathered = gather_blocks(params[member][layer_index], devices, turn % 3)
            weights[member] = gathered.reshape((-1, gathered.shape[-1]))
        for member, start, width in zip(narrow, starts, widths):
            weights[member] = small_all[:, layer_index, start : start + width].reshape(-1)
        weights_all.append(tuple(weights))
    stream = tokens
    saved_all = []
    for layer_index in range(LAYERS):
        shifted = layer_index % 2 == 1
        stream, saved_state = layer_forward(
            stream, weights_all[layer_index], shifted, rel_onehot, mask_add if shifted else None
        )
        saved_all.append(saved_state)
    result = stream * live_rows
    grad_stream = cotangent * live_rows
    layer_grads = [None] * LAYERS
    small_grads = [None] * LAYERS
    for layer_index in range(LAYERS - 1, -1, -1):
        shifted = layer_index % 2 == 1
        grad_stream, full_grads = layer_backward(
            grad_stream,
            saved_all[layer_index],
            weights_all[layer_index],
            shifted,
            rel_onehot,
            mask_add if shifted else None,
        )
        layer_grads[layer_index] = {}
        for turn, member in enumerate(wide):
            full = full_grads[member].astype(jnp.bfloat16)
            layer_grads[layer_index][member] = scatter_sums(
                full.reshape(devices, -1, full.shape[-1]), devices, turn % 3, jnp.bfloat16
            )
        small_grads[layer_index] = jnp.concatenate(
            [full_grads[member].reshape(devices, -1) for member in narrow], axis=1
        )
    small_sums = scatter_sums(jnp.stack(small_grads, axis=1), devices, 1, jnp.float32)
    finished = []
    for member in range(13):
        if member in wide:
            finished.append(jnp.stack([grads[member] for grads in layer_grads]))
        else:
            place = narrow.index(member)
            finished.append(small_sums[:, starts[place] : starts[place] + widths[place]])
    return (result, grad_stream) + tuple(finished)


def solution(mesh):
    in_specs = (
        P("fsdp", None, None),
        P("fsdp"),
        P(),
        P(),
        P(None, "fsdp"),
        P(None, "fsdp"),
        P(None, "fsdp", None),
        P(None, "fsdp"),
        P(None, "fsdp"),
        P(None, "fsdp", None),
        P(None, "fsdp"),
        P(None, "fsdp"),
        P(None, "fsdp"),
        P(None, "fsdp", None),
        P(None, "fsdp"),
        P(None, "fsdp", None),
        P(None, "fsdp"),
        P("fsdp", None, None),
    )
    out_specs = (
        P("fsdp", None, None),
        P("fsdp", None, None),
        P(None, "fsdp"),
        P(None, "fsdp"),
        P(None, "fsdp", None),
        P(None, "fsdp"),
        P(None, "fsdp"),
        P(None, "fsdp", None),
        P(None, "fsdp"),
        P(None, "fsdp"),
        P(None, "fsdp"),
        P(None, "fsdp", None),
        P(None, "fsdp"),
        P(None, "fsdp", None),
        P(None, "fsdp"),
    )
    devices = mesh.shape["fsdp"]
    return jax.shard_map(functools.partial(shards, devices), mesh=mesh, in_specs=in_specs, out_specs=out_specs, check_vma=False)
```

```python
import functools

import jax
import jax.numpy as jnp
from jax import lax
from jax.experimental import pallas as pl
from jax.experimental.pallas import tpu as pltpu
from jax.sharding import PartitionSpec as P

HEAD = 32
WIN = 7
GRID = 14
TABLE = 176
LAYERS = 2
HEADS = 16
SHIFT = 3


norm_eps = 1e-05
mask_fill = -100.0
ROWS = 64
GROUP = 128
PACK = GROUP // HEAD
empty_fill = -1e30


def to_windows(grid_rows):
    images = grid_rows.shape[0]
    features = grid_rows.shape[-1]
    split = grid_rows.reshape(images, GRID // WIN, WIN, GRID // WIN, WIN, features)
    split = split.transpose(0, 1, 3, 2, 4, 5)
    return split.reshape(images * (GRID // WIN) ** 2, WIN * WIN, features)


def from_windows(windows, images):
    features = windows.shape[-1]
    split = windows.reshape(images, GRID // WIN, GRID // WIN, WIN, WIN, features)
    split = split.transpose(0, 1, 3, 2, 4, 5)
    return split.reshape(images, GRID, GRID, features)


def enter_windows(token_rows, shifted):
    images = token_rows.shape[0]
    grid_rows = token_rows.reshape(images, GRID, GRID, token_rows.shape[-1])
    if shifted:
        grid_rows = jnp.roll(grid_rows, (-SHIFT, -SHIFT), axis=(1, 2))
    return to_windows(grid_rows)


def leave_windows(windows, images, shifted):
    grid_rows = from_windows(windows, images)
    if shifted:
        grid_rows = jnp.roll(grid_rows, (SHIFT, SHIFT), axis=(1, 2))
    return grid_rows.reshape(images, GRID * GRID, windows.shape[-1])


def layer_norm(stream, gain_row, offset):
    average = jnp.mean(stream, axis=-1, keepdims=True)
    centred = stream - average
    variance = jnp.mean(centred * centred, axis=-1, keepdims=True)
    return centred * lax.rsqrt(variance + norm_eps) * gain_row + offset


def gelu_exact(hidden):
    return jax.nn.gelu(hidden, approximate=False)


def contract_rows(rows_left, rows_right, precision=None):
    return lax.dot_general(
        rows_left,
        rows_right,
        (((0,), (0,)), ((), ())),
        precision=precision,
        preferred_element_type=jnp.float32,
    )


def times_transposed(rows_left, rows_right):
    return lax.dot_general(
        rows_left, rows_right, (((1,), (1,)), ((), ())), preferred_element_type=jnp.float32
    )


def position_bias(table_flat, rel_onehot):
    table_rows = table_flat.astype(jnp.float32).reshape(TABLE, HEADS)
    lookup = jnp.dot(
        rel_onehot, table_rows, precision=lax.Precision.HIGHEST, preferred_element_type=jnp.float32
    )
    return lookup.reshape(WIN * WIN, WIN * WIN, HEADS).transpose(2, 0, 1)


def window_rows(token_rows, shifted):
    windows = enter_windows(token_rows, shifted)
    windows = jnp.pad(windows, ((0, 0), (0, ROWS - WIN * WIN), (0, 0)))
    return windows.reshape(-1, windows.shape[-1])


def token_rows_of(rows, images, shifted):
    windows = rows.reshape(-1, ROWS, rows.shape[-1])[:, : WIN * WIN]
    return leave_windows(windows, images, shifted)


def padded_bias(table_flat, rel_onehot):
    bias = position_bias(table_flat, rel_onehot)
    spare = ROWS - WIN * WIN
    bias = jnp.pad(bias, ((0, 0), (0, spare), (0, 0)))
    bias = jnp.pad(bias, ((0, 0), (0, 0), (0, spare)), constant_values=empty_fill)
    return bias.reshape(HEADS * ROWS, ROWS)


def head_masks():
    lane = lax.broadcasted_iota(jnp.int32, (ROWS, GROUP), 1) // HEAD
    return [(lane == head).astype(jnp.float32) for head in range(PACK)]


def stack_heads(rows, masks):
    wide = rows.astype(jnp.float32)
    return jnp.concatenate([wide * mask for mask in masks], axis=0).astype(jnp.bfloat16)


def merge_heads(stacked, masks):
    total = stacked[:ROWS] * masks[0]
    for head in range(1, PACK):
        total = total + stacked[head * ROWS : (head + 1) * ROWS] * masks[head]
    return total


def dot_rows(left, right):
    return lax.dot_general(
        left, right, (((1,), (1,)), ((), ())), preferred_element_type=jnp.float32
    )


def group_probs(stacked, keys, bias_ref, mask_ref, group):
    scores = dot_rows(stacked, keys)
    scores = scores + bias_ref[group * PACK * ROWS : (group + 1) * PACK * ROWS, :]
    if mask_ref is not None:
        scores = scores + jnp.concatenate([mask_ref[0]] * PACK, axis=0)
    top = jnp.max(scores, axis=-1, keepdims=True)
    powers = jnp.exp(scores - top)
    return powers / jnp.sum(powers, axis=-1, keepdims=True)


def attend_kernel(features, has_mask, qkv_ref, bias_ref, *refs):
    mask_ref = refs[0] if has_mask else None
    out_ref = refs[-1]
    masks = head_masks()
    for group in range(features // GROUP):
        low = group * GROUP
        stacked = stack_heads(qkv_ref[:, low : low + GROUP], masks)
        keys = qkv_ref[:, features + low : features + low + GROUP]
        values = qkv_ref[:, 2 * features + low : 2 * features + low + GROUP]
        probs = group_probs(stacked, keys, bias_ref, mask_ref, group).astype(jnp.bfloat16)
        spread = jnp.dot(probs, values, preferred_element_type=jnp.float32)
        out_ref[:, low : low + GROUP] = merge_heads(spread, masks).astype(jnp.bfloat16)


def attend_back_kernel(features, has_mask, qkv_ref, grad_ref, bias_ref, *refs):
    mask_ref = refs[0] if has_mask else None
    out_ref, sums_ref, bias_grad_ref = refs[-3:]
    masks = head_masks()

    @pl.when(pl.program_id(0) == 0)
    def _():
        sums_ref[...] = jnp.zeros_like(sums_ref)
        bias_grad_ref[...] = jnp.zeros_like(bias_grad_ref)

    def put(part, low, value):
        at = part * features + low
        out_ref[:, at : at + GROUP] = value.astype(jnp.bfloat16)
        sums_ref[:, at : at + GROUP] += jnp.sum(value, axis=0, keepdims=True)

    for group in range(features // GROUP):
        low = group * GROUP
        rows = slice(group * PACK * ROWS, (group + 1) * PACK * ROWS)
        stacked = stack_heads(qkv_ref[:, low : low + GROUP], masks)
        grads = stack_heads(grad_ref[:, low : low + GROUP], masks)
        keys = qkv_ref[:, features + low : features + low + GROUP]
        values = qkv_ref[:, 2 * features + low : 2 * features + low + GROUP]
        probs = group_probs(stacked, keys, bias_ref, mask_ref, group)
        grad_probs = dot_rows(grads, values)
        grad_scores = probs * (
            grad_probs - jnp.sum(grad_probs * probs, axis=-1, keepdims=True)
        )
        bias_grad_ref[rows, :] += grad_scores
        low_scores = grad_scores.astype(jnp.bfloat16)
        put(2, low, contract_rows(probs.astype(jnp.bfloat16), grads))
        put(1, low, contract_rows(low_scores, stacked))
        spread = jnp.dot(low_scores, keys, preferred_element_type=jnp.float32)
        put(0, low, merge_heads(spread, masks) * HEAD ** (-0.5))


def attention_specs(features, bias_rows, mask_add):
    specs = [pl.BlockSpec((ROWS, 3 * features), lambda step: (step, 0))]
    last = [pl.BlockSpec(bias_rows.shape, lambda step: (0, 0))]
    operands = [bias_rows]
    if mask_add is not None:
        count = mask_add.shape[0]
        last.append(pl.BlockSpec((1, ROWS, ROWS), lambda step: (step % count, 0, 0)))
        operands.append(mask_add)
    return specs, last, operands


def attend_windows(qkv_low, bias_rows, mask_add):
    features = qkv_low.shape[1] // 3
    steps = qkv_low.shape[0] // ROWS
    first, last, operands = attention_specs(features, bias_rows, mask_add)
    return pl.pallas_call(
        functools.partial(attend_kernel, features, mask_add is not None),
        grid=(steps,),
        in_specs=first + last,
        out_specs=pl.BlockSpec((ROWS, features), lambda step: (step, 0)),
        out_shape=jax.ShapeDtypeStruct((steps * ROWS, features), jnp.bfloat16),
        compiler_params=pltpu.CompilerParams(vmem_limit_bytes=24 * 1024 * 1024),
        cost_estimate=pl.CostEstimate(flops=4 * steps * ROWS * ROWS * features * 4, bytes_accessed=8 * steps * ROWS * features, transcendentals=steps * HEADS * ROWS * ROWS),
    )(qkv_low, *operands)


def attend_windows_back(qkv_low, grad_low, bias_rows, mask_add):
    features = qkv_low.shape[1] // 3
    steps = qkv_low.shape[0] // ROWS
    first, last, operands = attention_specs(features, bias_rows, mask_add)
    return pl.pallas_call(
        functools.partial(attend_back_kernel, features, mask_add is not None),
        grid=(steps,),
        in_specs=first + [pl.BlockSpec((ROWS, features), lambda step: (step, 0))] + last,
        out_specs=(
            pl.BlockSpec((ROWS, 3 * features), lambda step: (step, 0)),
            pl.BlockSpec((1, 3 * features), lambda step: (0, 0)),
            pl.BlockSpec(bias_rows.shape, lambda step: (0, 0)),
        ),
        out_shape=(
            jax.ShapeDtypeStruct((steps * ROWS, 3 * features), jnp.bfloat16),
            jax.ShapeDtypeStruct((1, 3 * features), jnp.float32),
            jax.ShapeDtypeStruct(bias_rows.shape, jnp.float32),
        ),
        compiler_params=pltpu.CompilerParams(vmem_limit_bytes=24 * 1024 * 1024),
        cost_estimate=pl.CostEstimate(flops=10 * steps * ROWS * ROWS * features * 4, bytes_accessed=14 * steps * ROWS * features, transcendentals=steps * HEADS * ROWS * ROWS),
    )(qkv_low, grad_low, *operands)


def layer_forward(stream, weights, shifted, rel_onehot, mask_add):
    (
        gain_one,
        offset_one,
        qkv_w,
        qv_b,
        table_flat,
        proj_w,
        proj_b,
        gain_two,
        offset_two,
        up_w,
        up_b,
        down_w,
        down_b,
    ) = weights
    images = stream.shape[0]
    features = stream.shape[-1]
    normed_one = layer_norm(
        stream, gain_one.astype(jnp.float32), offset_one.astype(jnp.float32)
    ).astype(jnp.bfloat16)
    windows = window_rows(normed_one, shifted)
    qv_float = qv_b.astype(jnp.float32)
    head_scale = HEAD ** (-0.5)
    qkv = jnp.dot(windows, qkv_w, preferred_element_type=jnp.float32)
    qkv = qkv + jnp.concatenate(
        [qv_float[:features], jnp.zeros((features,), jnp.float32), qv_float[features:]]
    )
    qkv_scale = jnp.where(jnp.arange(3 * features) < features, head_scale, 1.0)
    qkv_low = (qkv * qkv_scale).astype(jnp.bfloat16)
    bias_rows = padded_bias(table_flat, rel_onehot)
    attended = attend_windows(qkv_low, bias_rows, mask_add)
    projected = jnp.dot(attended, proj_w, preferred_element_type=jnp.float32) + proj_b.astype(
        jnp.float32
    )
    stream_mid = stream + token_rows_of(projected, images, shifted)
    normed_two = layer_norm(
        stream_mid, gain_two.astype(jnp.float32), offset_two.astype(jnp.float32)
    ).astype(jnp.bfloat16)
    hidden_pre = jnp.dot(
        normed_two.reshape(-1, features), up_w, preferred_element_type=jnp.float32
    ) + up_b.astype(jnp.float32)
    activ_low = gelu_exact(hidden_pre).astype(jnp.bfloat16)
    branch_out = jnp.dot(activ_low, down_w, preferred_element_type=jnp.float32) + down_b.astype(
        jnp.float32
    )
    output = stream_mid + branch_out.reshape(stream.shape)
    saved_state = (
        stream,
        windows,
        qkv_low,
        bias_rows,
        attended,
        stream_mid,
        normed_two,
        hidden_pre,
        activ_low,
    )
    return (output, saved_state)


def layer_backward(grad_out, saved_state, weights, shifted, rel_onehot, mask_add):
    (
        gain_one,
        offset_one,
        qkv_w,
        qv_b,
        table_flat,
        proj_w,
        proj_b,
        gain_two,
        offset_two,
        up_w,
        up_b,
        down_w,
        down_b,
    ) = weights
    (
        stream,
        windows,
        qkv_low,
        bias_rows,
        attended,
        stream_mid,
        normed_two,
        hidden_pre,
        activ_low,
    ) = saved_state
    images = stream.shape[0]
    features = stream.shape[-1]
    grad_rows = grad_out.reshape(-1, features)
    grad_down_b = jnp.sum(grad_rows, axis=0)
    grad_low = grad_rows.astype(jnp.bfloat16)
    grad_down_w = contract_rows(activ_low, grad_low)
    grad_activ = times_transposed(grad_low, down_w)
    gelu_pull = jax.vjp(gelu_exact, hidden_pre)[1]
    grad_hidden = gelu_pull(grad_activ)[0]
    grad_up_b = jnp.sum(grad_hidden, axis=0)
    grad_hidden_low = grad_hidden.astype(jnp.bfloat16)
    grad_up_w = contract_rows(normed_two.reshape(-1, features), grad_hidden_low)
    grad_normed_two = times_transposed(grad_hidden_low, up_w).reshape(stream.shape)
    norm_pull = jax.vjp(
        layer_norm, stream_mid, gain_two.astype(jnp.float32), offset_two.astype(jnp.float32)
    )[1]
    part_mid, grad_gain_two, grad_offset_two = norm_pull(grad_normed_two)
    grad_mid = grad_out + part_mid
    grad_proj = window_rows(grad_mid, shifted)
    grad_proj_b = jnp.sum(grad_proj, axis=0)
    grad_proj_low = grad_proj.astype(jnp.bfloat16)
    grad_proj_w = contract_rows(attended, grad_proj_low)
    grad_attended = times_transposed(grad_proj_low, proj_w).astype(jnp.bfloat16)
    grad_qkv_low, qkv_sums, bias_sum = attend_windows_back(
        qkv_low, grad_attended, bias_rows, mask_add
    )
    bias_sum = bias_sum.reshape(HEADS, ROWS, ROWS)[:, : WIN * WIN, : WIN * WIN]
    bias_sum = bias_sum.transpose(1, 2, 0).reshape(WIN * WIN * WIN * WIN, HEADS)
    grad_table = contract_rows(rel_onehot, bias_sum, lax.Precision.HIGHEST).reshape(-1)
    grad_qv_b = jnp.concatenate([qkv_sums[0, :features], qkv_sums[0, 2 * features :]])
    grad_qkv_w = contract_rows(windows, grad_qkv_low)
    grad_normed_one = token_rows_of(times_transposed(grad_qkv_low, qkv_w), images, shifted)
    norm_pull = jax.vjp(
        layer_norm, stream, gain_one.astype(jnp.float32), offset_one.astype(jnp.float32)
    )[1]
    part_in, grad_gain_one, grad_offset_one = norm_pull(grad_normed_one)
    grad_in = grad_mid + part_in
    return (
        grad_in,
        (
            grad_gain_one,
            grad_offset_one,
            grad_qkv_w,
            grad_qv_b,
            grad_table,
            grad_proj_w,
            grad_proj_b,
            grad_gain_two,
            grad_offset_two,
            grad_up_w,
            grad_up_b,
            grad_down_w,
            grad_down_b,
        ),
    )


def bit_order(device_bits, turn):
    order = list(range(device_bits))
    if turn == 1 and device_bits > 2:
        order[1], order[2] = order[2], order[1]
    if turn == 2 and device_bits > 3:
        order[1:4] = [order[3], order[1], order[2]]
    return order


def partner_pairs(devices, bit):
    return [(place, place ^ (1 << bit)) for place in range(devices)]


def my_bit(bit):
    return (lax.axis_index("fsdp") >> bit) & 1


def gather_blocks(block, devices, turn):
    device_bits = devices.bit_length() - 1
    held = []
    for bit in reversed(bit_order(device_bits, turn)):
        other = lax.ppermute(block, "fsdp", partner_pairs(devices, bit))
        place = sum(1 for done in held if done > bit)
        held.append(bit)
        mine = my_bit(bit) == 0
        block = jnp.stack(
            [jnp.where(mine, block, other), jnp.where(mine, other, block)], axis=place
        )
    return block.reshape((devices,) + block.shape[device_bits:])


def scatter_sums(blocks, devices, turn, wire):
    device_bits = devices.bit_length() - 1
    rest = blocks.shape[1:]
    total = blocks.reshape((2,) * device_bits + rest)
    left = list(range(device_bits - 1, -1, -1))
    for bit in bit_order(device_bits, turn):
        axis = left.index(bit)
        left.remove(bit)
        mine = my_bit(bit)
        away = lax.dynamic_index_in_dim(total, 1 - mine, axis, keepdims=False).astype(wire)
        kept = lax.dynamic_index_in_dim(total, mine, axis, keepdims=False)
        arrived = lax.ppermute(away, "fsdp", partner_pairs(devices, bit))
        total = kept.astype(jnp.float32) + arrived.astype(jnp.float32)
        if left:
            total = total.astype(wire)
    return total


def shards(
    devices,
    tokens,
    live_count,
    rel_index,
    mask_ids,
    *params_and_cotangent,
):
    params = params_and_cotangent[:13]
    cotangent = params_and_cotangent[13]
    images = tokens.shape[0]
    live_rows = (jnp.arange(images) < live_count[0]).astype(jnp.float32)[:, None, None]
    rel_onehot = (rel_index.reshape(-1)[:, None] == jnp.arange(TABLE)[None, :]).astype(jnp.float32)
    region = to_windows(mask_ids.reshape(1, GRID, GRID, 1)).reshape(-1, WIN * WIN)
    mask_add = jnp.where(region[:, :, None] == region[:, None, :], 0.0, mask_fill).astype(
        jnp.float32
    )
    spare = ROWS - WIN * WIN
    mask_add = jnp.pad(mask_add, ((0, 0), (0, spare), (0, spare)))
    wide = (2, 5, 9, 11)
    narrow = tuple(member for member in range(13) if member not in wide)
    widths = [params[member].shape[1] for member in narrow]
    starts = [sum(widths[:place]) for place in range(len(widths))]
    small_all = gather_blocks(
        jnp.concatenate([params[member] for member in narrow], axis=1), devices, 1
    )
    weights_all = [[None] * 13 for _ in range(LAYERS)]
    for layer_index in range(LAYERS):
        for member, start, width in zip(narrow, starts, widths):
            weights_all[layer_index][member] = small_all[
                :, layer_index, start : start + width
            ].reshape(-1)
    before = small_all
    rounds = [(layer_index, group) for layer_index in range(LAYERS) for group in ((2, 5), (9, 11))]
    for layer_index, group in rounds:
        blocks = [params[member][layer_index] for member in group]
        if layer_index or group[0] != 2:
            before, *blocks = lax.optimization_barrier((before, *blocks))
        for turn, (member, block) in enumerate(zip(group, blocks)):
            gathered = gather_blocks(block, devices, (0, 2)[turn])
            weights_all[layer_index][member] = gathered.reshape((-1, gathered.shape[-1]))
        before = weights_all[layer_index][group[0]]
    stream = tokens
    saved_all = []
    for layer_index in range(LAYERS):
        shifted = layer_index % 2 == 1
        stream, saved_state = layer_forward(
            stream, weights_all[layer_index], shifted, rel_onehot, mask_add if shifted else None
        )
        saved_all.append(saved_state)
    result = stream * live_rows
    grad_stream = cotangent * live_rows
    layer_grads = [None] * LAYERS
    small_grads = [None] * LAYERS
    for layer_index in range(LAYERS - 1, -1, -1):
        shifted = layer_index % 2 == 1
        grad_stream, full_grads = layer_backward(
            grad_stream,
            saved_all[layer_index],
            weights_all[layer_index],
            shifted,
            rel_onehot,
            mask_add if shifted else None,
        )
        layer_grads[layer_index] = {}
        for turn, member in enumerate(wide):
            full = full_grads[member].astype(jnp.bfloat16)
            layer_grads[layer_index][member] = scatter_sums(
                full.reshape(devices, -1, full.shape[-1]), devices, turn % 3, jnp.bfloat16
            )
        small_grads[layer_index] = jnp.concatenate(
            [full_grads[member].reshape(devices, -1) for member in narrow], axis=1
        )
    small_sums = scatter_sums(jnp.stack(small_grads, axis=1), devices, 1, jnp.float32)
    finished = []
    for member in range(13):
        if member in wide:
            finished.append(jnp.stack([grads[member] for grads in layer_grads]))
        else:
            place = narrow.index(member)
            finished.append(small_sums[:, starts[place] : starts[place] + widths[place]])
    return (result, grad_stream) + tuple(finished)


def solution(mesh):
    in_specs = (
        P("fsdp", None, None),
        P("fsdp"),
        P(),
        P(),
        P(None, "fsdp"),
        P(None, "fsdp"),
        P(None, "fsdp", None),
        P(None, "fsdp"),
        P(None, "fsdp"),
        P(None, "fsdp", None),
        P(None, "fsdp"),
        P(None, "fsdp"),
        P(None, "fsdp"),
        P(None, "fsdp", None),
        P(None, "fsdp"),
        P(None, "fsdp", None),
        P(None, "fsdp"),
        P("fsdp", None, None),
    )
    out_specs = (
        P("fsdp", None, None),
        P("fsdp", None, None),
        P(None, "fsdp"),
        P(None, "fsdp"),
        P(None, "fsdp", None),
        P(None, "fsdp"),
        P(None, "fsdp"),
        P(None, "fsdp", None),
        P(None, "fsdp"),
        P(None, "fsdp"),
        P(None, "fsdp"),
        P(None, "fsdp", None),
        P(None, "fsdp"),
        P(None, "fsdp", None),
        P(None, "fsdp"),
    )
    devices = mesh.shape["fsdp"]
    return jax.shard_map(functools.partial(shards, devices), mesh=mesh, in_specs=in_specs, out_specs=out_specs, check_vma=False)
```

```python
import functools

import jax
import jax.numpy as jnp
from jax import lax
from jax.experimental import pallas as pl
from jax.experimental.pallas import tpu as pltpu
from jax.sharding import PartitionSpec as P

HEAD = 32
WIN = 7
GRID = 14
TABLE = 176
LAYERS = 2
HEADS = 16
SHIFT = 3


norm_eps = 1e-05
mask_fill = -100.0
ROWS = 64
GROUP = 128
PACK = GROUP // HEAD
empty_fill = -1e30


def to_windows(grid_rows):
    images = grid_rows.shape[0]
    features = grid_rows.shape[-1]
    split = grid_rows.reshape(images, GRID // WIN, WIN, GRID // WIN, WIN, features)
    split = split.transpose(0, 1, 3, 2, 4, 5)
    return split.reshape(images * (GRID // WIN) ** 2, WIN * WIN, features)


def from_windows(windows, images):
    features = windows.shape[-1]
    split = windows.reshape(images, GRID // WIN, GRID // WIN, WIN, WIN, features)
    split = split.transpose(0, 1, 3, 2, 4, 5)
    return split.reshape(images, GRID, GRID, features)


def enter_windows(token_rows, shifted):
    images = token_rows.shape[0]
    grid_rows = token_rows.reshape(images, GRID, GRID, token_rows.shape[-1])
    if shifted:
        grid_rows = jnp.roll(grid_rows, (-SHIFT, -SHIFT), axis=(1, 2))
    return to_windows(grid_rows)


def leave_windows(windows, images, shifted):
    grid_rows = from_windows(windows, images)
    if shifted:
        grid_rows = jnp.roll(grid_rows, (SHIFT, SHIFT), axis=(1, 2))
    return grid_rows.reshape(images, GRID * GRID, windows.shape[-1])


def layer_norm(stream, gain_row, offset):
    average = jnp.mean(stream, axis=-1, keepdims=True)
    centred = stream - average
    variance = jnp.mean(centred * centred, axis=-1, keepdims=True)
    return centred * lax.rsqrt(variance + norm_eps) * gain_row + offset


def gelu_exact(hidden):
    return jax.nn.gelu(hidden, approximate=False)


def contract_rows(rows_left, rows_right, precision=None):
    return lax.dot_general(
        rows_left,
        rows_right,
        (((0,), (0,)), ((), ())),
        precision=precision,
        preferred_element_type=jnp.float32,
    )


def times_transposed(rows_left, rows_right):
    return lax.dot_general(
        rows_left, rows_right, (((1,), (1,)), ((), ())), preferred_element_type=jnp.float32
    )


def position_bias(table_flat, rel_onehot):
    table_rows = table_flat.astype(jnp.float32).reshape(TABLE, HEADS)
    lookup = jnp.dot(
        rel_onehot, table_rows, precision=lax.Precision.HIGHEST, preferred_element_type=jnp.float32
    )
    return lookup.reshape(WIN * WIN, WIN * WIN, HEADS).transpose(2, 0, 1)


def window_rows(token_rows, shifted):
    windows = enter_windows(token_rows, shifted)
    windows = jnp.pad(windows, ((0, 0), (0, ROWS - WIN * WIN), (0, 0)))
    return windows.reshape(-1, windows.shape[-1])


def token_rows_of(rows, images, shifted):
    windows = rows.reshape(-1, ROWS, rows.shape[-1])[:, : WIN * WIN]
    return leave_windows(windows, images, shifted)


def padded_bias(table_flat, rel_onehot):
    bias = position_bias(table_flat, rel_onehot)
    spare = ROWS - WIN * WIN
    bias = jnp.pad(bias, ((0, 0), (0, spare), (0, 0)))
    bias = jnp.pad(bias, ((0, 0), (0, 0), (0, spare)), constant_values=empty_fill)
    return bias.reshape(HEADS * ROWS, ROWS)


def head_masks():
    lane = lax.broadcasted_iota(jnp.int32, (ROWS, GROUP), 1) // HEAD
    return [(lane == head).astype(jnp.float32) for head in range(PACK)]


def stack_heads(rows, masks):
    wide = rows.astype(jnp.float32)
    return jnp.concatenate([wide * mask for mask in masks], axis=0).astype(jnp.bfloat16)


def merge_heads(stacked, masks):
    total = stacked[:ROWS] * masks[0]
    for head in range(1, PACK):
        total = total + stacked[head * ROWS : (head + 1) * ROWS] * masks[head]
    return total


def dot_rows(left, right):
    return lax.dot_general(
        left, right, (((1,), (1,)), ((), ())), preferred_element_type=jnp.float32
    )


def group_probs(stacked, keys, bias_ref, mask_ref, group):
    scores = dot_rows(stacked, keys)
    scores = scores + bias_ref[group * PACK * ROWS : (group + 1) * PACK * ROWS, :]
    if mask_ref is not None:
        scores = scores + jnp.concatenate([mask_ref[0]] * PACK, axis=0)
    top = jnp.max(scores, axis=-1, keepdims=True)
    powers = jnp.exp(scores - top)
    return powers / jnp.sum(powers, axis=-1, keepdims=True)


def attend_kernel(features, has_mask, qkv_ref, bias_ref, *refs):
    mask_ref = refs[0] if has_mask else None
    out_ref = refs[-1]
    masks = head_masks()
    for group in range(features // GROUP):
        low = group * GROUP
        stacked = stack_heads(qkv_ref[:, low : low + GROUP], masks)
        keys = qkv_ref[:, features + low : features + low + GROUP]
        values = qkv_ref[:, 2 * features + low : 2 * features + low + GROUP]
        probs = group_probs(stacked, keys, bias_ref, mask_ref, group).astype(jnp.bfloat16)
        spread = jnp.dot(probs, values, preferred_element_type=jnp.float32)
        out_ref[:, low : low + GROUP] = merge_heads(spread, masks).astype(jnp.bfloat16)


def attend_back_kernel(features, has_mask, qkv_ref, grad_ref, bias_ref, *refs):
    mask_ref = refs[0] if has_mask else None
    out_ref, sums_ref, bias_grad_ref = refs[-3:]
    masks = head_masks()

    @pl.when(pl.program_id(0) == 0)
    def _():
        sums_ref[...] = jnp.zeros_like(sums_ref)
        bias_grad_ref[...] = jnp.zeros_like(bias_grad_ref)

    def put(part, low, value):
        at = part * features + low
        out_ref[:, at : at + GROUP] = value.astype(jnp.bfloat16)
        sums_ref[:, at : at + GROUP] += jnp.sum(value, axis=0, keepdims=True)

    for group in range(features // GROUP):
        low = group * GROUP
        rows = slice(group * PACK * ROWS, (group + 1) * PACK * ROWS)
        stacked = stack_heads(qkv_ref[:, low : low + GROUP], masks)
        grads = stack_heads(grad_ref[:, low : low + GROUP], masks)
        keys = qkv_ref[:, features + low : features + low + GROUP]
        values = qkv_ref[:, 2 * features + low : 2 * features + low + GROUP]
        probs = group_probs(stacked, keys, bias_ref, mask_ref, group)
        grad_probs = dot_rows(grads, values)
        grad_scores = probs * (
            grad_probs - jnp.sum(grad_probs * probs, axis=-1, keepdims=True)
        )
        bias_grad_ref[rows, :] += grad_scores
        low_scores = grad_scores.astype(jnp.bfloat16)
        put(2, low, contract_rows(probs.astype(jnp.bfloat16), grads))
        put(1, low, contract_rows(low_scores, stacked))
        spread = jnp.dot(low_scores, keys, preferred_element_type=jnp.float32)
        put(0, low, merge_heads(spread, masks) * HEAD ** (-0.5))


def attention_specs(features, bias_rows, mask_add):
    specs = [pl.BlockSpec((ROWS, 3 * features), lambda step: (step, 0))]
    last = [pl.BlockSpec(bias_rows.shape, lambda step: (0, 0))]
    operands = [bias_rows]
    if mask_add is not None:
        count = mask_add.shape[0]
        last.append(pl.BlockSpec((1, ROWS, ROWS), lambda step: (step % count, 0, 0)))
        operands.append(mask_add)
    return specs, last, operands


def attend_windows(qkv_low, bias_rows, mask_add):
    features = qkv_low.shape[1] // 3
    steps = qkv_low.shape[0] // ROWS
    first, last, operands = attention_specs(features, bias_rows, mask_add)
    return pl.pallas_call(
        functools.partial(attend_kernel, features, mask_add is not None),
        grid=(steps,),
        in_specs=first + last,
        out_specs=pl.BlockSpec((ROWS, features), lambda step: (step, 0)),
        out_shape=jax.ShapeDtypeStruct((steps * ROWS, features), jnp.bfloat16),
        compiler_params=pltpu.CompilerParams(vmem_limit_bytes=24 * 1024 * 1024),
        cost_estimate=pl.CostEstimate(flops=4 * steps * ROWS * ROWS * features * 4, bytes_accessed=8 * steps * ROWS * features, transcendentals=steps * HEADS * ROWS * ROWS),
    )(qkv_low, *operands)


def attend_windows_back(qkv_low, grad_low, bias_rows, mask_add):
    features = qkv_low.shape[1] // 3
    steps = qkv_low.shape[0] // ROWS
    first, last, operands = attention_specs(features, bias_rows, mask_add)
    return pl.pallas_call(
        functools.partial(attend_back_kernel, features, mask_add is not None),
        grid=(steps,),
        in_specs=first + [pl.BlockSpec((ROWS, features), lambda step: (step, 0))] + last,
        out_specs=(
            pl.BlockSpec((ROWS, 3 * features), lambda step: (step, 0)),
            pl.BlockSpec((1, 3 * features), lambda step: (0, 0)),
            pl.BlockSpec(bias_rows.shape, lambda step: (0, 0)),
        ),
        out_shape=(
            jax.ShapeDtypeStruct((steps * ROWS, 3 * features), jnp.bfloat16),
            jax.ShapeDtypeStruct((1, 3 * features), jnp.float32),
            jax.ShapeDtypeStruct(bias_rows.shape, jnp.float32),
        ),
        compiler_params=pltpu.CompilerParams(vmem_limit_bytes=24 * 1024 * 1024),
        cost_estimate=pl.CostEstimate(flops=10 * steps * ROWS * ROWS * features * 4, bytes_accessed=14 * steps * ROWS * features, transcendentals=steps * HEADS * ROWS * ROWS),
    )(qkv_low, grad_low, *operands)


def layer_forward(stream, weights, shifted, rel_onehot, mask_add):
    (
        gain_one,
        offset_one,
        qkv_w,
        qv_b,
        table_flat,
        proj_w,
        proj_b,
        gain_two,
        offset_two,
        up_w,
        up_b,
        down_w,
        down_b,
    ) = weights
    images = stream.shape[0]
    features = stream.shape[-1]
    normed_one = layer_norm(
        stream, gain_one.astype(jnp.float32), offset_one.astype(jnp.float32)
    ).astype(jnp.bfloat16)
    windows = window_rows(normed_one, shifted)
    qv_float = qv_b.astype(jnp.float32)
    head_scale = HEAD ** (-0.5)
    qkv = jnp.dot(windows, qkv_w, preferred_element_type=jnp.float32)
    qkv = qkv + jnp.concatenate(
        [qv_float[:features], jnp.zeros((features,), jnp.float32), qv_float[features:]]
    )
    qkv_scale = jnp.where(jnp.arange(3 * features) < features, head_scale, 1.0)
    qkv_low = (qkv * qkv_scale).astype(jnp.bfloat16)
    bias_rows = padded_bias(table_flat, rel_onehot)
    attended = attend_windows(qkv_low, bias_rows, mask_add)
    projected = jnp.dot(attended, proj_w, preferred_element_type=jnp.float32) + proj_b.astype(
        jnp.float32
    )
    stream_mid = stream + token_rows_of(projected, images, shifted)
    normed_two = layer_norm(
        stream_mid, gain_two.astype(jnp.float32), offset_two.astype(jnp.float32)
    ).astype(jnp.bfloat16)
    hidden_pre = jnp.dot(
        normed_two.reshape(-1, features), up_w, preferred_element_type=jnp.float32
    ) + up_b.astype(jnp.float32)
    activ_low = gelu_exact(hidden_pre).astype(jnp.bfloat16)
    branch_out = jnp.dot(activ_low, down_w, preferred_element_type=jnp.float32) + down_b.astype(
        jnp.float32
    )
    output = stream_mid + branch_out.reshape(stream.shape)
    saved_state = (
        stream,
        windows,
        qkv_low,
        bias_rows,
        attended,
        stream_mid,
        normed_two,
        hidden_pre,
        activ_low,
    )
    return (output, saved_state)


def layer_backward(grad_out, saved_state, weights, shifted, rel_onehot, mask_add):
    (
        gain_one,
        offset_one,
        qkv_w,
        qv_b,
        table_flat,
        proj_w,
        proj_b,
        gain_two,
        offset_two,
        up_w,
        up_b,
        down_w,
        down_b,
    ) = weights
    (
        stream,
        windows,
        qkv_low,
        bias_rows,
        attended,
        stream_mid,
        normed_two,
        hidden_pre,
        activ_low,
    ) = saved_state
    images = stream.shape[0]
    features = stream.shape[-1]
    grad_rows = grad_out.reshape(-1, features)
    grad_down_b = jnp.sum(grad_rows, axis=0)
    grad_low = grad_rows.astype(jnp.bfloat16)
    grad_down_w = contract_rows(activ_low, grad_low)
    grad_activ = times_transposed(grad_low, down_w)
    gelu_pull = jax.vjp(gelu_exact, hidden_pre)[1]
    grad_hidden = gelu_pull(grad_activ)[0]
    grad_up_b = jnp.sum(grad_hidden, axis=0)
    grad_hidden_low = grad_hidden.astype(jnp.bfloat16)
    grad_up_w = contract_rows(normed_two.reshape(-1, features), grad_hidden_low)
    grad_normed_two = times_transposed(grad_hidden_low, up_w).reshape(stream.shape)
    norm_pull = jax.vjp(
        layer_norm, stream_mid, gain_two.astype(jnp.float32), offset_two.astype(jnp.float32)
    )[1]
    part_mid, grad_gain_two, grad_offset_two = norm_pull(grad_normed_two)
    grad_mid = grad_out + part_mid
    grad_mid, grad_up_w, grad_down_w = lax.optimization_barrier(
        (grad_mid, grad_up_w.astype(jnp.bfloat16), grad_down_w.astype(jnp.bfloat16))
    )
    grad_proj = window_rows(grad_mid, shifted)
    grad_proj_b = jnp.sum(grad_proj, axis=0)
    grad_proj_low = grad_proj.astype(jnp.bfloat16)
    grad_proj_w = contract_rows(attended, grad_proj_low)
    grad_attended = times_transposed(grad_proj_low, proj_w).astype(jnp.bfloat16)
    grad_qkv_low, qkv_sums, bias_sum = attend_windows_back(
        qkv_low, grad_attended, bias_rows, mask_add
    )
    bias_sum = bias_sum.reshape(HEADS, ROWS, ROWS)[:, : WIN * WIN, : WIN * WIN]
    bias_sum = bias_sum.transpose(1, 2, 0).reshape(WIN * WIN * WIN * WIN, HEADS)
    grad_table = contract_rows(rel_onehot, bias_sum, lax.Precision.HIGHEST).reshape(-1)
    grad_qv_b = jnp.concatenate([qkv_sums[0, :features], qkv_sums[0, 2 * features :]])
    grad_qkv_w = contract_rows(windows, grad_qkv_low)
    grad_normed_one = token_rows_of(times_transposed(grad_qkv_low, qkv_w), images, shifted)
    norm_pull = jax.vjp(
        layer_norm, stream, gain_one.astype(jnp.float32), offset_one.astype(jnp.float32)
    )[1]
    part_in, grad_gain_one, grad_offset_one = norm_pull(grad_normed_one)
    grad_in = grad_mid + part_in
    return (
        grad_in,
        (
            grad_gain_one,
            grad_offset_one,
            grad_qkv_w,
            grad_qv_b,
            grad_table,
            grad_proj_w,
            grad_proj_b,
            grad_gain_two,
            grad_offset_two,
            grad_up_w,
            grad_up_b,
            grad_down_w,
            grad_down_b,
        ),
    )


def bit_order(device_bits, turn):
    order = list(range(device_bits))
    if turn == 1 and device_bits > 2:
        order[1], order[2] = order[2], order[1]
    if turn == 2 and device_bits > 3:
        order[1:4] = [order[3], order[1], order[2]]
    return order


def partner_pairs(devices, bit):
    return [(place, place ^ (1 << bit)) for place in range(devices)]


def my_bit(bit):
    return (lax.axis_index("fsdp") >> bit) & 1


def gather_blocks(block, devices, turn):
    device_bits = devices.bit_length() - 1
    held = []
    for bit in reversed(bit_order(device_bits, turn)):
        other = lax.ppermute(block, "fsdp", partner_pairs(devices, bit))
        place = sum(1 for done in held if done > bit)
        held.append(bit)
        mine = my_bit(bit) == 0
        block = jnp.stack(
            [jnp.where(mine, block, other), jnp.where(mine, other, block)], axis=place
        )
    return block.reshape((devices,) + block.shape[device_bits:])


def scatter_sums(blocks, devices, turn, wire):
    device_bits = devices.bit_length() - 1
    rest = blocks.shape[1:]
    total = blocks.reshape((2,) * device_bits + rest)
    left = list(range(device_bits - 1, -1, -1))
    for bit in bit_order(device_bits, turn):
        axis = left.index(bit)
        left.remove(bit)
        mine = my_bit(bit)
        away = lax.dynamic_index_in_dim(total, 1 - mine, axis, keepdims=False).astype(wire)
        kept = lax.dynamic_index_in_dim(total, mine, axis, keepdims=False)
        arrived = lax.ppermute(away, "fsdp", partner_pairs(devices, bit))
        total = kept.astype(jnp.float32) + arrived.astype(jnp.float32)
        if left:
            total = total.astype(wire)
    return total


def shards(
    devices,
    tokens,
    live_count,
    rel_index,
    mask_ids,
    *params_and_cotangent,
):
    params = params_and_cotangent[:13]
    cotangent = params_and_cotangent[13]
    images = tokens.shape[0]
    live_rows = (jnp.arange(images) < live_count[0]).astype(jnp.float32)[:, None, None]
    rel_onehot = (rel_index.reshape(-1)[:, None] == jnp.arange(TABLE)[None, :]).astype(jnp.float32)
    region = to_windows(mask_ids.reshape(1, GRID, GRID, 1)).reshape(-1, WIN * WIN)
    mask_add = jnp.where(region[:, :, None] == region[:, None, :], 0.0, mask_fill).astype(
        jnp.float32
    )
    spare = ROWS - WIN * WIN
    mask_add = jnp.pad(mask_add, ((0, 0), (0, spare), (0, spare)))
    wide = (2, 5, 9, 11)
    narrow = tuple(member for member in range(13) if member not in wide)
    widths = [params[member].shape[1] for member in narrow]
    starts = [sum(widths[:place]) for place in range(len(widths))]
    small_all = gather_blocks(
        jnp.concatenate([params[member] for member in narrow], axis=1), devices, 1
    )
    weights_all = [[None] * 13 for _ in range(LAYERS)]
    for layer_index in range(LAYERS):
        for member, start, width in zip(narrow, starts, widths):
            weights_all[layer_index][member] = small_all[
                :, layer_index, start : start + width
            ].reshape(-1)
    before = small_all
    rounds = [(layer_index, group) for layer_index in range(LAYERS) for group in ((2, 5), (9, 11))]
    for layer_index, group in rounds:
        blocks = [params[member][layer_index] for member in group]
        if layer_index or group[0] != 2:
            before, *blocks = lax.optimization_barrier((before, *blocks))
        for turn, (member, block) in enumerate(zip(group, blocks)):
            gathered = gather_blocks(block, devices, (0, 2)[turn])
            weights_all[layer_index][member] = gathered.reshape((-1, gathered.shape[-1]))
        before = weights_all[layer_index][group[0]]
    stream = tokens
    saved_all = []
    for layer_index in range(LAYERS):
        shifted = layer_index % 2 == 1
        stream, saved_state = layer_forward(
            stream, weights_all[layer_index], shifted, rel_onehot, mask_add if shifted else None
        )
        saved_all.append(saved_state)
    result = stream * live_rows
    grad_stream = cotangent * live_rows
    layer_grads = [None] * LAYERS
    small_grads = [None] * LAYERS
    for layer_index in range(LAYERS - 1, -1, -1):
        shifted = layer_index % 2 == 1
        grad_stream, full_grads = layer_backward(
            grad_stream,
            saved_all[layer_index],
            weights_all[layer_index],
            shifted,
            rel_onehot,
            mask_add if shifted else None,
        )
        layer_grads[layer_index] = {}
        for turn, member in enumerate(wide):
            full = full_grads[member].astype(jnp.bfloat16)
            layer_grads[layer_index][member] = scatter_sums(
                full.reshape(devices, -1, full.shape[-1]), devices, turn % 3, jnp.bfloat16
            )
        small_grads[layer_index] = jnp.concatenate(
            [full_grads[member].reshape(devices, -1) for member in narrow], axis=1
        )
    small_sums = scatter_sums(jnp.stack(small_grads, axis=1), devices, 1, jnp.float32)
    finished = []
    for member in range(13):
        if member in wide:
            finished.append(jnp.stack([grads[member] for grads in layer_grads]))
        else:
            place = narrow.index(member)
            finished.append(small_sums[:, starts[place] : starts[place] + widths[place]])
    return (result, grad_stream) + tuple(finished)


def solution(mesh):
    in_specs = (
        P("fsdp", None, None),
        P("fsdp"),
        P(),
        P(),
        P(None, "fsdp"),
        P(None, "fsdp"),
        P(None, "fsdp", None),
        P(None, "fsdp"),
        P(None, "fsdp"),
        P(None, "fsdp", None),
        P(None, "fsdp"),
        P(None, "fsdp"),
        P(None, "fsdp"),
        P(None, "fsdp", None),
        P(None, "fsdp"),
        P(None, "fsdp", None),
        P(None, "fsdp"),
        P("fsdp", None, None),
    )
    out_specs = (
        P("fsdp", None, None),
        P("fsdp", None, None),
        P(None, "fsdp"),
        P(None, "fsdp"),
        P(None, "fsdp", None),
        P(None, "fsdp"),
        P(None, "fsdp"),
        P(None, "fsdp", None),
        P(None, "fsdp"),
        P(None, "fsdp"),
        P(None, "fsdp"),
        P(None, "fsdp", None),
        P(None, "fsdp"),
        P(None, "fsdp", None),
        P(None, "fsdp"),
    )
    devices = mesh.shape["fsdp"]
    return jax.shard_map(functools.partial(shards, devices), mesh=mesh, in_specs=in_specs, out_specs=out_specs, check_vma=False)
```
